256 devices in a mesh: row: 8 (over x, core), col: 8 (over y, z_lo), depth: 4 (over z_hi).
Axes of the slice: x: 4, y: 4, z: 8 (z_hi: 4, z_lo: 2; z = z_hi * 2 + z_lo), core: 2. Of those that a mesh axis runs over, the one named last changes fastest.
Arguments:
- inputs: bfloat16 [2048, 8192], P('col', ('depth', 'row')), may hold values from -6 to 6
- query_weight: bfloat16 [8192, 8192], P('depth', ('row', 'col')), may hold values from -0.0625 to 0.0625
- keyval_weight: bfloat16 [8192, 2048], P('depth', ('row', 'col')), may hold values from -0.0625 to 0.0625
- output_weight: bfloat16 [8192, 8192], P('row', ('depth', 'col')), may hold values from -0.0625 to 0.0625
- cotangent: bfloat16 [2048, 8192], P('col', ('depth', 'row')), may hold values from -3 to 3
- query_moment: float32 [8192, 8192], P('depth', ('row', 'col')), may hold values from -6 to 6
- query_second: float32 [8192, 8192], P('depth', ('row', 'col')), may hold values from 1 to 100
- keyval_moment: float32 [8192, 2048], P('depth', ('row', 'col')), may hold values from -6 to 6
- keyval_second: float32 [8192, 2048], P('depth', ('row', 'col')), may hold values from 1 to 100
- output_moment: float32 [8192, 8192], P('row', ('depth', 'col')), may hold values from -6 to 6
- output_second: float32 [8192, 8192], P('row', ('depth', 'col')), may hold values from 1 to 100
Outputs:
- grad_input: bfloat16 [2048, 8192], P('col', ('depth', 'row'))
- next_query_weight: bfloat16 [8192, 8192], P('depth', ('row', 'col'))
- next_query_moment: float32 [8192, 8192], P('depth', ('row', 'col'))
- next_query_second: float32 [8192, 8192], P('depth', ('row', 'col'))
- next_keyval_weight: bfloat16 [8192, 2048], P('depth', ('row', 'col'))
- next_keyval_moment: float32 [8192, 2048], P('depth', ('row', 'col'))
- next_keyval_second: float32 [8192, 2048], P('depth', ('row', 'col'))
- next_output_weight: bfloat16 [8192, 8192], P('row', ('depth', 'col'))
- next_output_moment: float32 [8192, 8192], P('row', ('depth', 'col'))
- next_output_second: float32 [8192, 8192], P('row', ('depth', 'col'))
The draws below stay inside these ranges and needn't reach their ends.
All inputs are finite; a program needn't handle non-finite values.
Results may differ from the reference program's by a relative error of at most 0.028.
Values may be sent and summed in bfloat16 or wider, within the bound.
No kernel may reach another device: no remote copies, remote signals or barrier semaphores. Data moves between devices by JAX's collectives and lax.ppermute only.
A program may use at most 128 MiB of HBM per device.

```python
import math
import jax
import jax.numpy as jnp
from jax import lax

D = 8192
HQ = 64
KVH = 8
HD = 128
TOK_DEV = 256
SEQ = 2048
QDIM = 8192
KVDIM = 2048
GROUP = 8
N_COL = 8


def block_scale(stream_key, dims, shards, low, high):
    level, own = 1.0, jax.random.fold_in(stream_key, 6)
    for position, blocks in shards:
        steps = jnp.exp(jax.random.uniform(jax.random.fold_in(own, position), (blocks,), jnp.float32, low / len(shards), high / len(shards)))
        level = level * jnp.repeat(steps, dims[position] // blocks).reshape([-1 if axis == position else 1 for axis in range(len(dims))])
    return level


def scatter_about(own_key, dims, spread, limit, shards=(), dtype=jnp.bfloat16):
    values = spread * jax.random.normal(own_key, dims, jnp.float32)
    if shards:
        values = values * block_scale(own_key, dims, shards, -0.22, 0.18)
    return jnp.clip(values, -limit, limit).astype(dtype)


def setup_inputs(seed: int = 0) -> dict:
    seeds = jax.random.split(jax.random.key(seed), 12)
    return {
        "inputs": scatter_about(seeds[0], (SEQ, D), 1.0, 6.0, ((0, 8), (1, 32))),
        "query_weight": scatter_about(seeds[1], (D, QDIM), D ** -0.5, 0.0625, ((0, 4), (1, 64))),
        "keyval_weight": scatter_about(seeds[2], (D, KVDIM), D ** -0.5, 0.0625, ((0, 4), (1, 64))),
        "output_weight": scatter_about(seeds[3], (QDIM, D), QDIM ** -0.5, 0.0625, ((0, 8), (1, 32))),
        "cotangent": scatter_about(seeds[4], (SEQ, D), 0.5, 3.0, ((0, 8), (1, 32))),
        "query_moment": scatter_about(seeds[5], (D, QDIM), 1.0, 6.0, ((0, 4), (1, 64)), jnp.float32),
        "query_second": jnp.clip(jnp.exp(math.log(100.0) - 4.6051702 * jax.random.uniform(seeds[6], (D, QDIM), jnp.float32) ** block_scale(seeds[6], (D, QDIM), ((0, 4), (1, 64)), -0.2, 0.2)), 1.0, 100.0),
        "keyval_moment": scatter_about(seeds[7], (D, KVDIM), 1.0, 6.0, ((0, 4), (1, 64)), jnp.float32),
        "keyval_second": jnp.clip(jnp.exp(math.log(100.0) - 4.6051702 * jax.random.uniform(seeds[8], (D, KVDIM), jnp.float32) ** block_scale(seeds[8], (D, KVDIM), ((0, 4), (1, 64)), -0.2, 0.2)), 1.0, 100.0),
        "output_moment": scatter_about(seeds[9], (QDIM, D), 1.0, 6.0, ((0, 8), (1, 32)), jnp.float32),
        "output_second": jnp.clip(jnp.exp(math.log(100.0) - 4.6051702 * jax.random.uniform(seeds[10], (QDIM, D), jnp.float32) ** block_scale(seeds[10], (QDIM, D), ((0, 8), (1, 32)), -0.2, 0.2)), 1.0, 100.0),
    }


beta_one = 0.9
beta_two = 0.95
learn_rate = 0.001
adam_count = 100
epsilon = 1e-08

def adam_update(weight, moment, second, gradient):
    moment_next = beta_one * moment + (1.0 - beta_one) * gradient
    second_next = beta_two * second + (1.0 - beta_two) * gradient * gradient
    corrected = moment_next / (1.0 - beta_one ** adam_count)
    scaled = jnp.sqrt(second_next / (1.0 - beta_two ** adam_count)) + epsilon
    weight_next = (weight.astype(jnp.float32) - learn_rate * corrected / scaled).astype(jnp.bfloat16)
    return (weight_next, moment_next, second_next)

def block_grad(left, right):
    total = jnp.zeros((left.shape[1], right.shape[1]), jnp.float32)
    for block in range(N_COL):
        left_piece = left[block * TOK_DEV:(block + 1) * TOK_DEV]
        right_piece = right[block * TOK_DEV:(block + 1) * TOK_DEV]
        partial_value = jnp.dot(left_piece.T, right_piece, preferred_element_type=jnp.float32)
        rounded = lax.optimization_barrier(partial_value.astype(jnp.bfloat16))
        total = total + rounded.astype(jnp.float32)
    return total

def reference(inputs, query_weight, keyval_weight, output_weight, cotangent, query_moment, query_second, keyval_moment, keyval_second, output_moment, output_second):
    scale_factor = 1.0 / math.sqrt(HD)
    queries = jnp.dot(inputs, query_weight, preferred_element_type=jnp.float32).astype(jnp.bfloat16)
    keyval = jnp.dot(inputs, keyval_weight, preferred_element_type=jnp.float32).astype(jnp.bfloat16)
    grad_heads = jnp.dot(cotangent, output_weight.T, preferred_element_type=jnp.float32).astype(jnp.bfloat16)
    paired = keyval.reshape(SEQ, KVH, 2, HD)
    key_heads = jnp.repeat(paired[:, :, 0, :].transpose(1, 0, 2), GROUP, axis=0)
    value_heads = jnp.repeat(paired[:, :, 1, :].transpose(1, 0, 2), GROUP, axis=0)
    query_heads = queries.reshape(SEQ, HQ, HD).transpose(1, 0, 2)
    grad_out_heads = grad_heads.reshape(SEQ, HQ, HD).transpose(1, 0, 2)
    positions = lax.iota(jnp.int32, SEQ)
    visible = positions[None, :] <= positions[:, None]

    def head_pass(operands):
        query, key, value, grad_out = operands
        scores = jnp.dot(query, key.T, preferred_element_type=jnp.float32) * scale_factor
        raised = jnp.where(visible, jnp.exp(jnp.where(visible, scores, 0.0)), 0.0)
        probs = raised / lax.optimization_barrier(jnp.sum(raised, axis=1, keepdims=True))
        probs_low = probs.astype(jnp.bfloat16)
        head_out = jnp.dot(probs_low, value, preferred_element_type=jnp.float32).astype(jnp.bfloat16)
        prob_grads = jnp.dot(grad_out, value.T, preferred_element_type=jnp.float32)
        delta_rows = lax.optimization_barrier(jnp.sum(probs * prob_grads, axis=1, keepdims=True))
        score_grads = (probs * (prob_grads - delta_rows)).astype(jnp.bfloat16)
        query_grad = (jnp.dot(score_grads, key, preferred_element_type=jnp.float32) * scale_factor).astype(jnp.bfloat16)
        key_part = jnp.dot(score_grads.T, query, preferred_element_type=jnp.float32) * scale_factor
        value_part = jnp.dot(probs_low.T, grad_out, preferred_element_type=jnp.float32)
        return (head_out, query_grad, key_part, value_part)
    head_out, query_grad, key_part, value_part = lax.map(head_pass, (query_heads, key_heads, value_heads, grad_out_heads))
    head_flat = head_out.transpose(1, 0, 2).reshape(SEQ, QDIM)
    grad_queries = query_grad.transpose(1, 0, 2).reshape(SEQ, QDIM)
    key_total = lax.optimization_barrier(jnp.sum(key_part.reshape(KVH, GROUP, SEQ, HD), axis=1))
    value_total = lax.optimization_barrier(jnp.sum(value_part.reshape(KVH, GROUP, SEQ, HD), axis=1))
    keyval_grads = jnp.stack([key_total, value_total], axis=1).transpose(2, 0, 1, 3).reshape(SEQ, KVDIM).astype(jnp.bfloat16)
    grad_input = (jnp.dot(grad_queries, query_weight.T, preferred_element_type=jnp.float32) + jnp.dot(keyval_grads, keyval_weight.T, preferred_element_type=jnp.float32)).astype(jnp.bfloat16)
    output_gradient = block_grad(head_flat, cotangent)
    query_gradient = block_grad(inputs, grad_queries)
    keyval_gradient = block_grad(inputs, keyval_grads)
    query_next = adam_update(query_weight, query_moment, query_second, query_gradient)
    keyval_next = adam_update(keyval_weight, keyval_moment, keyval_second, keyval_gradient)
    output_next = adam_update(output_weight, output_moment, output_second, output_gradient)
    return (grad_input, query_next[0], query_next[1], query_next[2], keyval_next[0], keyval_next[1], keyval_next[2], output_next[0], output_next[1], output_next[2])
```

```python
import math

import jax
import jax.numpy as jnp
from jax import lax
from jax.experimental import pallas as pl
from jax.experimental.pallas import tpu as pltpu
from jax.sharding import PartitionSpec as P

HD = 128
SCALE = 1.0 / math.sqrt(HD)
F32 = jnp.float32
BF16 = jnp.bfloat16

beta_one = 0.9
beta_two = 0.95
learn_rate = 0.001
adam_count = 100
epsilon = 1e-08

CORE_SWAP = [(r, r ^ 1) for r in range(8)]
ZLO_SWAP = [(c, c ^ 1) for c in range(8)]


def ring(axis, step):
    if axis == "x":
        return "row", [(r, ((r // 2 + step) % 4) * 2 + r % 2) for r in range(8)]
    if axis == "y":
        return "col", [(c, ((c // 2 + step) % 4) * 2 + c % 2) for c in range(8)]
    return "depth", [(d, (d + step) % 4) for d in range(4)]


def send(value, axis, step):
    name, pairs = ring(axis, step)
    return lax.ppermute(value, name, pairs)


def gather4(value, axis):
    from_left = send(value, axis, 1)
    from_right = send(value, axis, 3)
    across = send(value, axis, 2)
    return [value, from_right, across, from_left]


def scatter4(pieces, axis):
    right = send(pieces[1], axis, 1)
    left = send(pieces[3], axis, 3)
    across = send(pieces[2], axis, 2)
    return [pieces[0], right, across, left]


def total(parts):
    result = parts[0].astype(F32)
    for part in parts[1:]:
        result = result + part.astype(F32)
    return result


def nt(left, right):
    return lax.dot_general(left, right, (((1,), (1,)), ((), ())), preferred_element_type=F32)


def tn(left, right):
    return lax.dot_general(left, right, (((0,), (0,)), ((), ())), preferred_element_type=F32)


def nn(left, right):
    return jnp.dot(left, right, preferred_element_type=F32)


def at(stack, *index):
    rest = stack.shape[len(index) :]
    piece = lax.dynamic_slice(
        stack, tuple(index) + (0,) * len(rest), (1,) * len(index) + rest
    )
    return piece.reshape(rest)


def adam_update(weight, moment, second, gradient):
    moment_next = beta_one * moment + (1.0 - beta_one) * gradient
    second_next = beta_two * second + (1.0 - beta_two) * gradient * gradient
    corrected = moment_next / (1.0 - beta_one**adam_count)
    scaled = jnp.sqrt(second_next / (1.0 - beta_two**adam_count)) + epsilon
    weight_next = (weight.astype(F32) - learn_rate * corrected / scaled).astype(BF16)
    return (weight_next, moment_next, second_next)


def attention_kernel(at_ref, q_ref, g_ref, kv_ref, o_ref, dq_ref, dkv_ref, kt, vt, dkt, dvt):
    y_at, zlo_at, zhi_at = at_ref[0], at_ref[1], at_ref[2]

    def places():
        for source in range(8):
            y_source, zlo_source = divmod(source, 2)
            rows = pl.ds((y_source % 2) * 64, 64)
            for half in range(2):
                for step in range(4):
                    block = ((y_source + step) % 4) * 2 + zlo_source
                    there = pl.ds(block * 256 + half * 128, 128)
                    here = pl.ds((half * 4 + step) * 128, 128)
                    yield source, y_source, rows, there, here

    for source, y_source, rows, there, here in places():
        target = kt if y_source < 2 else vt
        target[rows, there] = kv_ref[source, :, here]

    row_id = lax.broadcasted_iota(jnp.int32, (128, 1), 0)
    for block in (3, 2, 1, 0):
        keys = (2 * block + 2) * 256
        step = lax.rem(block - y_at + 4, 4)

        def rows_of(ref):
            first, last = ref[step], ref[4 + step]
            return jnp.concatenate(
                [first[:, :HD], first[:, HD:], last[:, :HD], last[:, HD:]], axis=0
            )

        query, grad = rows_of(q_ref), rows_of(g_ref)
        key_t, value_t = kt[:, :keys], vt[:, :keys]
        query_pos = (2 * block + zlo_at) * 256 + (row_id // 64) * 128 + zhi_at * 32 + row_id % 32
        key_pos = lax.broadcasted_iota(jnp.int32, (128, keys), 1)
        scores = nn(query, key_t) * SCALE
        raised = jnp.where(key_pos <= query_pos, jnp.exp(scores), 0.0)
        probs = raised * (1.0 / jnp.sum(raised, axis=1, keepdims=True))
        probs_low = probs.astype(BF16)
        out = nt(probs_low, value_t).astype(BF16)
        prob_grads = nn(grad, value_t)
        delta = jnp.sum(probs * prob_grads, axis=1, keepdims=True)
        score_grads = (probs * (prob_grads - delta)).astype(BF16)
        grad_query = (nt(score_grads, key_t) * SCALE).astype(BF16)
        key_part = tn(query, score_grads)
        value_part = tn(grad, probs_low)
        if block == 3:
            dkt[...] = key_part
            dvt[...] = value_part
        else:
            dkt[:, :keys] += key_part
            dvt[:, :keys] += value_part
        for ref, value in ((o_ref, out), (dq_ref, grad_query)):
            ref[step] = jnp.concatenate([value[:32], value[32:64]], axis=1)
            ref[4 + step] = jnp.concatenate([value[64:96], value[96:]], axis=1)

    for source, y_source, rows, there, here in places():
        if y_source < 2:
            dkv_ref[source, :, here] = (dkt[rows, there] * SCALE).astype(BF16)
        else:
            dkv_ref[source, :, here] = dvt[rows, there].astype(BF16)


def attention(place, queries, grads, keyval):
    return pl.pallas_call(
        attention_kernel,
        out_shape=(
            jax.ShapeDtypeStruct(queries.shape, BF16),
            jax.ShapeDtypeStruct(queries.shape, BF16),
            jax.ShapeDtypeStruct(keyval.shape, BF16),
        ),
        in_specs=[
            pl.BlockSpec(memory_space=pltpu.SMEM),
            pl.BlockSpec(memory_space=pltpu.VMEM),
            pl.BlockSpec(memory_space=pltpu.VMEM),
            pl.BlockSpec(memory_space=pltpu.VMEM),
        ],
        out_specs=[pl.BlockSpec(memory_space=pltpu.VMEM)] * 3,
        scratch_shapes=[
            pltpu.VMEM((HD, 2048), BF16),
            pltpu.VMEM((HD, 2048), BF16),
            pltpu.VMEM((HD, 2048), F32),
            pltpu.VMEM((HD, 2048), F32),
        ],
        compiler_params=pltpu.CompilerParams(vmem_limit_bytes=28 * 1024 * 1024),
    )(place, queries, grads, keyval)


def gather_tokens(block):
    first, last = block[:128], block[128:]
    first_x = jnp.concatenate(gather4(first, "x"), axis=1)
    last_y = jnp.concatenate(gather4(last, "y"), axis=0)
    first_all = jnp.concatenate(gather4(first_x, "y"), axis=0)
    last_all = jnp.concatenate(gather4(last_y, "x"), axis=1)
    return first_all, last_all


def on_device(
    inputs,
    query_weight,
    keyval_weight,
    output_weight,
    cotangent,
    query_moment,
    query_second,
    keyval_moment,
    keyval_second,
    output_moment,
    output_second,
):
    row_at = lax.axis_index("row")
    col_at = lax.axis_index("col")
    zhi_at = lax.axis_index("depth")
    x_at, core_at = row_at // 2, row_at % 2
    y_at, zlo_at = col_at // 2, col_at % 2
    low = zlo_at == 0

    def mod4(value):
        return lax.rem(value + 4, 4)

    def zlo_swap(value):
        return lax.ppermute(value, "col", ZLO_SWAP)

    def core_swap(value):
        return lax.ppermute(value, "row", CORE_SWAP)

    def in_order(own, other):
        return jnp.where(low, own, other), jnp.where(low, other, own)

    own_halves = gather_tokens(inputs)
    feats = [list(own_halves), [core_swap(half) for half in own_halves]]

    query_pair = jnp.concatenate(in_order(query_weight, zlo_swap(query_weight)), axis=1)
    keyval_t = keyval_weight.T
    keyval_pair = jnp.concatenate(in_order(keyval_t, zlo_swap(keyval_t)), axis=0)
    query_stack = query_pair.reshape(4, 2, 256, 256)
    keyval_stack = keyval_pair.reshape(64, 8, 256)
    query_rel, keyval_rel = [], []
    for side in range(2):
        core = core_at ^ side
        query_rel.append(
            jnp.concatenate([at(query_stack, mod4(x_at + j - 4), core) for j in range(4)], axis=0)
        )
        keyval_rel.append(
            jnp.concatenate(
                [
                    lax.dynamic_slice(
                        keyval_pair, (0, (mod4(x_at + j - 4) * 2 + core) * 256), (64, 256)
                    )
                    for j in range(4)
                ],
                axis=1,
            )
        )

    head_rows = output_weight.reshape(4, 256, 256)
    came = scatter4([at(head_rows, mod4(y_at + j - 4)) for j in range(4)], "y")
    own_cols = jnp.stack([came[0], came[3], came[2], came[1]])
    col_stack = jnp.stack([own_cols, zlo_swap(own_cols)])
    output_rel = []
    for side in range(2):
        which = core_at ^ side ^ zlo_at
        output_rel.append(
            jnp.concatenate(
                [at(col_stack, which, mod4(x_at + j - y_at)) for j in range(4)], axis=1
            )
        )

    def to_owner(halves):
        parts = jnp.stack(halves).reshape(8, 4, 32, 256)
        pieces = []
        for j in range(4):
            piece = lax.dynamic_slice(
                parts, (0, mod4(zhi_at + j - 4), 0, 0), (8, 1, 32, 256)
            ).reshape(8, 32, 256)
            pieces.append(piece if j == 0 else piece.astype(BF16))
        return total(scatter4(pieces, "z")).astype(BF16)

    keyval_part = jnp.concatenate(
        [
            nt(keyval_rel[0], feats[0][half]) + nt(keyval_rel[1], feats[1][half])
            for half in range(2)
        ],
        axis=1,
    ).astype(BF16)
    keyval_own = total(gather4(keyval_part, "z")).astype(BF16)
    keyval_all = lax.all_to_all(
        jnp.broadcast_to(keyval_own[None], (8, 64, 1024)), "col", 0, 0, tiled=True
    )
    queries = to_owner(
        [
            nn(feats[0][half], query_rel[0]) + nn(feats[1][half], query_rel[1])
            for half in range(2)
        ]
    )

    own_halves = gather_tokens(cotangent)
    cots = [list(own_halves), [core_swap(half) for half in own_halves]]
    grad_heads = to_owner(
        [
            nt(cots[0][half], output_rel[0]) + nt(cots[1][half], output_rel[1])
            for half in range(2)
        ]
    )

    place = jnp.stack([y_at, zlo_at, zhi_at]).astype(jnp.int32)
    head_out, grad_queries, keyval_parts = attention(place, queries, grad_heads, keyval_all)

    def all_rows(own):
        near = jnp.stack(gather4(own, "z"))
        rows = jnp.stack([at(near, mod4(d - zhi_at)) for d in range(4)], axis=1)
        return rows.reshape(2, 512, 256)

    keyval_came = lax.all_to_all(keyval_parts, "col", 0, 0, tiled=True)
    keyval_sum = jnp.sum(keyval_came.astype(F32), axis=0).astype(BF16)
    query_rows = all_rows(grad_queries)
    keyval_grads = total(gather4(keyval_sum, "z")).astype(BF16)
    keyval_halves = [keyval_grads[:, :512], keyval_grads[:, 512:]]

    def input_part(side, half):
        return nt(query_rows[half], query_rel[side]) + tn(keyval_halves[half], keyval_rel[side])

    sums = []
    for half in range(2):
        theirs = core_swap(input_part(1, half).astype(BF16))
        sums.append((input_part(0, half) + theirs.astype(F32)).astype(BF16))
    first = sums[0].reshape(4, 128, 1024)
    first = total(scatter4([first[j] for j in range(4)], "y")).astype(BF16)
    last = sums[1].reshape(512, 4, 256)
    last = total(scatter4([last[:, j] for j in range(4)], "x")).astype(BF16)
    first = total(scatter4([first[:, 256 * j : 256 * (j + 1)] for j in range(4)], "x"))
    last = total(scatter4([last[128 * j : 128 * (j + 1)] for j in range(4)], "y"))
    grad_input = jnp.concatenate([first, last], axis=0).astype(BF16)

    head_rows_all = all_rows(head_out)
    output_parts = []
    for side in range(2):
        part = tn(head_rows_all[0], cots[side][0]) + tn(head_rows_all[1], cots[side][1])
        output_parts.append(
            jnp.stack([part.astype(BF16)[:, 256 * j : 256 * (j + 1)] for j in range(4)])
        )
    output_parts = jnp.stack(output_parts)
    mine = core_at ^ zlo_at
    output_sum = (
        at(output_parts, mine).astype(F32) + zlo_swap(at(output_parts, mine ^ 1)).astype(F32)
    ).astype(BF16)
    came = scatter4([at(output_sum, mod4(y_at + j - x_at)) for j in range(4)], "y")
    came = jnp.stack([came[0], came[3], came[2], came[1]])
    output_gradient = jnp.concatenate([at(came, mod4(j - y_at)) for j in range(4)], axis=0)

    query_parts = []
    for side in range(2):
        part = tn(feats[side][0], query_rows[0]) + tn(feats[side][1], query_rows[1])
        query_parts.append(part.astype(BF16).reshape(4, 256, 256))
    query_parts = jnp.stack(query_parts)
    query_kept = jnp.where(low, query_parts[..., :HD], query_parts[..., HD:])
    query_sent = jnp.where(low, query_parts[..., HD:], query_parts[..., :HD])
    query_sum = query_kept.astype(F32) + zlo_swap(query_sent).astype(F32)
    query_gradient = jnp.concatenate(
        [at(query_sum, core_at ^ c, mod4(j - x_at)) for j in range(4) for c in range(2)], axis=0
    )

    keyval_grad_parts = []
    for side in range(2):
        keyval_grad_parts.append(
            (
                nn(keyval_halves[0], feats[side][0]) + nn(keyval_halves[1], feats[side][1])
            ).astype(BF16)
        )
    keyval_grad_parts = jnp.concatenate(keyval_grad_parts, axis=1)
    keyval_kept = jnp.where(low, keyval_grad_parts[:32], keyval_grad_parts[32:])
    keyval_sent = jnp.where(low, keyval_grad_parts[32:], keyval_grad_parts[:32])
    keyval_total = keyval_kept.astype(F32) + zlo_swap(keyval_sent).astype(F32)
    keyval_gradient = jnp.concatenate(
        [
            lax.dynamic_slice(
                keyval_total, (0, ((core_at ^ c) * 4 + mod4(j - x_at)) * 256), (32, 256)
            )
            for j in range(4)
            for c in range(2)
        ],
        axis=1,
    ).T

    query_next = adam_update(query_weight, query_moment, query_second, query_gradient)
    keyval_next = adam_update(keyval_weight, keyval_moment, keyval_second, keyval_gradient)
    output_next = adam_update(
        output_weight, output_moment, output_second, output_gradient.astype(F32)
    )
    return (grad_input, *query_next, *keyval_next, *output_next)


def solution(mesh):
    placed = (
        P("col", ("depth", "row")),
        P("depth", ("row", "col")),
        P("depth", ("row", "col")),
        P("row", ("depth", "col")),
        P("col", ("depth", "row")),
        P("depth", ("row", "col")),
        P("depth", ("row", "col")),
        P("depth", ("row", "col")),
        P("depth", ("row", "col")),
        P("row", ("depth", "col")),
        P("row", ("depth", "col")),
    )
    return jax.shard_map(
        on_device,
        mesh=mesh,
        in_specs=placed,
        out_specs=(
            P("col", ("depth", "row")),
            P("depth", ("row", "col")),
            P("depth", ("row", "col")),
            P("depth", ("row", "col")),
            P("depth", ("row", "col")),
            P("depth", ("row", "col")),
            P("depth", ("row", "col")),
            P("row", ("depth", "col")),
            P("row", ("depth", "col")),
            P("row", ("depth", "col")),
        ),
        check_vma=False,
    )
```

```python
import math

import jax
import jax.numpy as jnp
from jax import lax
from jax.experimental import pallas as pl
from jax.experimental.pallas import tpu as pltpu
from jax.sharding import Mesh
from jax.sharding import PartitionSpec as P

HD = 128
SCALE = 1.0 / math.sqrt(HD)
F32 = jnp.float32
BF16 = jnp.bfloat16

beta_one = 0.9
beta_two = 0.95
learn_rate = 0.001
adam_count = 100
epsilon = 1e-08

SIZES = (4, 2, 4, 2, 4)
NAMES = ("x", "core", "y", "zlo", "zhi")


def send(value, axis, step):
    return lax.ppermute(value, axis, [(i, (i + step) % 4) for i in range(4)])


def swap(value, axis):
    return lax.ppermute(value, axis, [(0, 1), (1, 0)])


def gather4(value, axis):
    from_left = send(value, axis, 1)
    from_right = send(value, axis, 3)
    across = send(value, axis, 2)
    return [value, from_right, across, from_left]


def scatter4(pieces, axis):
    right = send(pieces[1], axis, 1)
    left = send(pieces[3], axis, 3)
    across = send(pieces[2], axis, 2)
    return [pieces[0], right, across, left]


def after(value, *events):
    return lax.optimization_barrier((value, *events))[0]


def total(parts):
    result = parts[0].astype(F32)
    for part in parts[1:]:
        result = result + part.astype(F32)
    return result


def nt(left, right):
    return lax.dot_general(left, right, (((1,), (1,)), ((), ())), preferred_element_type=F32)


def tn(left, right):
    return lax.dot_general(left, right, (((0,), (0,)), ((), ())), preferred_element_type=F32)


def nn(left, right):
    return jnp.dot(left, right, preferred_element_type=F32)


def at(stack, *index):
    rest = stack.shape[len(index) :]
    piece = lax.dynamic_slice(
        stack, tuple(index) + (0,) * len(rest), (1,) * len(index) + rest
    )
    return piece.reshape(rest)


def adam_update(weight, moment, second, gradient):
    moment_next = beta_one * moment + (1.0 - beta_one) * gradient
    second_next = beta_two * second + (1.0 - beta_two) * gradient * gradient
    corrected = moment_next / (1.0 - beta_one**adam_count)
    scaled = jnp.sqrt(second_next / (1.0 - beta_two**adam_count)) + epsilon
    weight_next = (weight.astype(F32) - learn_rate * corrected / scaled).astype(BF16)
    return (weight_next, moment_next, second_next)


def attention_kernel(at_ref, q_ref, g_ref, kv_ref, o_ref, dq_ref, dkv_ref, kt, vt, dkt, dvt):
    y_at, zlo_at, zhi_at = at_ref[0], at_ref[1], at_ref[2]

    def places():
        for y_source in range(4):
            rows = pl.ds((y_source % 2) * 64, 64)
            near = lax.rem(y_source - y_at + 4, 4)
            for zlo in range(2):
                for half in range(2):
                    for step in range(4):
                        block = ((y_source + step) % 4) * 2 + zlo
                        there = pl.ds(block * 256 + half * 128, 128)
                        here = pl.ds((half * 4 + step) * 128, 128)
                        yield y_source, near, zlo, rows, there, here

    for y_source, near, zlo, rows, there, here in places():
        target = kt if y_source < 2 else vt
        target[rows, there] = kv_ref[near, zlo, :, here]

    def load(ref, first, last):
        first, last = ref[first], ref[last]
        return jnp.concatenate(
            [first[:, :HD], first[:, HD:], last[:, :HD], last[:, HD:]], axis=0
        )

    def store(ref, first, last, value):
        ref[first] = jnp.concatenate([value[:32], value[32:64]], axis=1)
        ref[last] = jnp.concatenate([value[64:96], value[96:]], axis=1)

    row_id = lax.broadcasted_iota(jnp.int32, (128, 1), 0)
    for block in (3, 2, 1, 0):
        keys = (2 * block + 2) * 256
        step = lax.rem(block - y_at + 4, 4)
        query = load(q_ref, step, 4 + step)
        grad = load(g_ref, 2 * block, 2 * block + 1)
        key_t, value_t = kt[:, :keys], vt[:, :keys]
        query_pos = (2 * block + zlo_at) * 256 + (row_id // 64) * 128 + zhi_at * 32 + row_id % 32
        key_pos = lax.broadcasted_iota(jnp.int32, (128, keys), 1)
        scores = nn(query, key_t) * SCALE
        raised = jnp.where(key_pos <= query_pos, jnp.exp(scores), 0.0)
        probs = raised * (1.0 / jnp.sum(raised, axis=1, keepdims=True))
        probs_low = probs.astype(BF16)
        out = nt(probs_low, value_t).astype(BF16)
        prob_grads = nn(grad, value_t)
        delta = jnp.sum(probs * prob_grads, axis=1, keepdims=True)
        score_grads = (probs * (prob_grads - delta)).astype(BF16)
        grad_query = (nt(score_grads, key_t) * SCALE).astype(BF16)
        key_part = tn(query, score_grads)
        value_part = tn(grad, probs_low)
        if block == 3:
            dkt[...] = key_part
            dvt[...] = value_part
        else:
            dkt[:, :keys] += key_part
            dvt[:, :keys] += value_part
        store(o_ref, 2 * block, 2 * block + 1, out)
        store(dq_ref, step, 4 + step, grad_query)

    for y_source, near, zlo, rows, there, here in places():
        if y_source < 2:
            dkv_ref[near, zlo, :, here] = (dkt[rows, there] * SCALE).astype(BF16)
        else:
            dkv_ref[near, zlo, :, here] = dvt[rows, there].astype(BF16)


def attention(place, queries, grads, keyval):
    return pl.pallas_call(
        attention_kernel,
        out_shape=(
            jax.ShapeDtypeStruct(queries.shape, BF16),
            jax.ShapeDtypeStruct(queries.shape, BF16),
            jax.ShapeDtypeStruct(keyval.shape, BF16),
        ),
        in_specs=[
            pl.BlockSpec(memory_space=pltpu.SMEM),
            pl.BlockSpec(memory_space=pltpu.VMEM),
            pl.BlockSpec(memory_space=pltpu.VMEM),
            pl.BlockSpec(memory_space=pltpu.VMEM),
        ],
        out_specs=[pl.BlockSpec(memory_space=pltpu.VMEM)] * 3,
        scratch_shapes=[
            pltpu.VMEM((HD, 2048), BF16),
            pltpu.VMEM((HD, 2048), BF16),
            pltpu.VMEM((HD, 2048), F32),
            pltpu.VMEM((HD, 2048), F32),
        ],
        compiler_params=pltpu.CompilerParams(vmem_limit_bytes=28 * 1024 * 1024),
    )(place, queries, grads, keyval)


def on_device(
    inputs,
    query_weight,
    keyval_weight,
    output_weight,
    cotangent,
    query_moment,
    query_second,
    keyval_moment,
    keyval_second,
    output_moment,
    output_second,
):
    x_at, core_at = lax.axis_index("x"), lax.axis_index("core")
    y_at, zlo_at = lax.axis_index("y"), lax.axis_index("zlo")
    zhi_at = lax.axis_index("zhi")
    low = zlo_at == 0

    def mod4(value):
        return lax.rem(value + 4, 4)

    def in_order(own, other):
        return jnp.where(low, own, other), jnp.where(low, other, own)

    cot_own = lax.all_gather(cotangent, ("x", "y"), axis=0, tiled=True)

    first, last = inputs[:128], inputs[128:]
    first_x = jnp.concatenate(gather4(first, "x"), axis=1)
    last_y = jnp.concatenate(gather4(last, "y"), axis=0)
    own_halves = [
        jnp.concatenate(gather4(first_x, "y"), axis=0),
        jnp.concatenate(gather4(last_y, "x"), axis=1),
    ]
    feats = [own_halves, [swap(half, "core") for half in own_halves]]

    query_pair = jnp.concatenate(in_order(query_weight, swap(query_weight, "zlo")), axis=1)
    keyval_t = keyval_weight.T
    keyval_pair = jnp.concatenate(in_order(keyval_t, swap(keyval_t, "zlo")), axis=0)
    query_stack = query_pair.reshape(4, 2, 256, 256)
    query_rel, keyval_rel, joined_rel = [], [], []
    for side in range(2):
        core = core_at ^ side
        query_rel.append(
            jnp.concatenate([at(query_stack, mod4(x_at + j - 4), core) for j in range(4)], axis=0)
        )
        keyval_rel.append(
            jnp.concatenate(
                [
                    lax.dynamic_slice(
                        keyval_pair, (0, (mod4(x_at + j - 4) * 2 + core) * 256), (64, 256)
                    )
                    for j in range(4)
                ],
                axis=1,
            )
        )
        joined_rel.append(jnp.concatenate([query_rel[side], keyval_rel[side].T], axis=1))

    head_rows = after(output_weight, first_x, last_y).reshape(4, 256, 256)
    came = scatter4([at(head_rows, mod4(y_at + j - 4)) for j in range(4)], "y")
    own_cols = jnp.stack([came[0], came[3], came[2], came[1]])
    col_stack = jnp.stack([own_cols, swap(own_cols, "zlo")])
    output_cols = [
        [at(col_stack, core_at ^ side ^ zlo_at, mod4(j - y_at)) for j in range(4)]
        for side in range(2)
    ]

    def to_owner(parts):
        pieces = []
        for j in range(4):
            piece = lax.dynamic_slice(
                parts, (0, mod4(zhi_at + j - 4), 0, 0), (8, 1, 32, 256)
            ).reshape(8, 32, 256)
            pieces.append(piece if j == 0 else piece.astype(BF16))
        return total(scatter4(pieces, "zhi")).astype(BF16)

    keyval_part = jnp.concatenate(
        [
            nt(keyval_rel[0], feats[0][half]) + nt(keyval_rel[1], feats[1][half])
            for half in range(2)
        ],
        axis=1,
    ).astype(BF16)
    keyval_own = total(gather4(keyval_part, "zhi")).astype(BF16)
    keyval_both = jnp.stack(in_order(keyval_own, swap(keyval_own, "zlo")))
    keyval_all = jnp.stack(gather4(keyval_both, "y"))
    queries = to_owner(
        jnp.stack(
            [
                nn(feats[0][half], query_rel[0]) + nn(feats[1][half], query_rel[1])
                for half in range(2)
            ]
        ).reshape(8, 4, 32, 256)
    )

    cots = [side.reshape(4, 1024, 256) for side in (cot_own, swap(cot_own, "core"))]
    grad_part = None
    for side in range(2):
        for j in range(4):
            term = nt(cots[side][j], output_cols[side][j])
            grad_part = term if grad_part is None else grad_part + term
    grad_heads = to_owner(grad_part.reshape(8, 4, 32, 256))

    place = jnp.stack([y_at, zlo_at, zhi_at]).astype(jnp.int32)
    head_out, grad_queries, keyval_parts = attention(place, queries, grad_heads, keyval_all)

    def all_rows(own):
        near = jnp.stack(gather4(own, "zhi"))
        rows = jnp.stack([at(near, mod4(d - zhi_at)) for d in range(4)], axis=1)
        return rows.reshape(1024, 256)

    keyval_came = total(scatter4([keyval_parts[j] for j in range(4)], "y"))
    keyval_came = keyval_came.astype(BF16)
    keyval_kept = jnp.where(low, keyval_came[0], keyval_came[1])
    keyval_sent = jnp.where(low, keyval_came[1], keyval_came[0])
    query_rows = all_rows(grad_queries)
    keyval_sum = total([keyval_kept, swap(keyval_sent, "zlo")]).astype(BF16)
    keyval_grads = total(gather4(keyval_sum, "zhi")).astype(BF16)

    joined = jnp.concatenate([query_rows, keyval_grads.T], axis=1)
    sums = []
    for half in range(2):
        rows = joined[512 * half : 512 * (half + 1)]
        theirs = swap(nt(rows, joined_rel[1]).astype(BF16), "core")
        sums.append((nt(rows, joined_rel[0]) + theirs.astype(F32)).astype(BF16))
    first = sums[0].reshape(4, 128, 1024)
    first = total(scatter4([first[j] for j in range(4)], "y")).astype(BF16)
    last = sums[1].reshape(512, 4, 256)
    last = total(scatter4([last[:, j] for j in range(4)], "x")).astype(BF16)
    first = total(scatter4([first[:, 256 * j : 256 * (j + 1)] for j in range(4)], "x"))
    last = total(scatter4([last[128 * j : 128 * (j + 1)] for j in range(4)], "y"))
    grad_input = jnp.concatenate([first, last], axis=0).astype(BF16)

    query_rows, head_out = lax.optimization_barrier((query_rows, head_out, keyval_grads))[:2]
    query_halves = [query_rows[:512], query_rows[512:]]
    query_parts = []
    for side in range(2):
        part = tn(feats[side][0], query_halves[0]) + tn(feats[side][1], query_halves[1])
        query_parts.append(part.astype(BF16).reshape(4, 256, 256))
    query_parts = jnp.stack(query_parts)
    query_kept = jnp.where(low, query_parts[..., :HD], query_parts[..., HD:])
    query_sent = jnp.where(low, query_parts[..., HD:], query_parts[..., :HD])
    query_sum = query_kept.astype(F32) + swap(query_sent, "zlo").astype(F32)
    query_gradient = jnp.concatenate(
        [at(query_sum, core_at ^ c, mod4(j - x_at)) for j in range(4) for c in range(2)], axis=0
    )

    head_rows_all = all_rows(head_out)
    output_parts = jnp.stack(
        [
            jnp.stack([tn(head_rows_all, cots[side][j]).astype(BF16) for j in range(4)])
            for side in range(2)
        ]
    )
    mine = core_at ^ zlo_at
    output_sum = total([at(output_parts, mine), swap(at(output_parts, mine ^ 1), "zlo")])
    output_sum = output_sum.astype(BF16)
    came = scatter4([at(output_sum, mod4(y_at + j - 4)) for j in range(4)], "y")
    came = jnp.stack([came[0], came[3], came[2], came[1]])
    output_gradient = jnp.concatenate([at(came, mod4(j - y_at)) for j in range(4)], axis=0)

    keyval_halves = [keyval_grads[:, :512], keyval_grads[:, 512:]]
    keyval_grad_parts = []
    for side in range(2):
        keyval_grad_parts.append(
            (
                nn(keyval_halves[0], feats[side][0]) + nn(keyval_halves[1], feats[side][1])
            ).astype(BF16)
        )
    keyval_grad_parts = jnp.concatenate(keyval_grad_parts, axis=1)
    keyval_kept = jnp.where(low, keyval_grad_parts[:32], keyval_grad_parts[32:])
    keyval_sent = jnp.where(low, keyval_grad_parts[32:], keyval_grad_parts[:32])
    keyval_total = keyval_kept.astype(F32) + swap(keyval_sent, "zlo").astype(F32)
    keyval_gradient = jnp.concatenate(
        [
            lax.dynamic_slice(
                keyval_total, (0, ((core_at ^ c) * 4 + mod4(j - x_at)) * 256), (32, 256)
            )
            for j in range(4)
            for c in range(2)
        ],
        axis=1,
    ).T

    query_next = adam_update(query_weight, query_moment, query_second, query_gradient)
    keyval_next = adam_update(keyval_weight, keyval_moment, keyval_second, keyval_gradient)
    output_next = adam_update(
        output_weight, output_moment, output_second, output_gradient.astype(F32)
    )
    return (grad_input, *query_next, *keyval_next, *output_next)


def solution(mesh):
    fine = Mesh(mesh.devices.reshape(SIZES), NAMES)
    tokens = P(("y", "zlo"), ("zhi", "x", "core"))
    heads = P("zhi", ("x", "core", "y", "zlo"))
    output = P(("x", "core"), ("zhi", "y", "zlo"))
    return jax.shard_map(
        on_device,
        mesh=fine,
        in_specs=(tokens, heads, heads, output, tokens, *[heads] * 4, output, output),
        out_specs=(tokens, *[heads] * 6, *[output] * 3),
        check_vma=False,
    )
```

```python
import math

import jax
import jax.numpy as jnp
from jax import lax
from jax.experimental import pallas as pl
from jax.experimental.pallas import tpu as pltpu
from jax.sharding import Mesh
from jax.sharding import PartitionSpec as P

HD = 128
SCALE = 1.0 / math.sqrt(HD)
F32 = jnp.float32
BF16 = jnp.bfloat16

beta_one = 0.9
beta_two = 0.95
learn_rate = 0.001
adam_count = 100
epsilon = 1e-08

SIZES = (4, 2, 4, 2, 4)
NAMES = ("x", "core", "y", "zlo", "zhi")


def send(value, axis, step):
    return lax.ppermute(value, axis, [(i, (i + step) % 4) for i in range(4)])


def swap(value, axis):
    return lax.ppermute(value, axis, [(0, 1), (1, 0)])


def gather4(value, axis):
    from_left = send(value, axis, 1)
    from_right = send(value, axis, 3)
    across = send(value, axis, 2)
    return [value, from_right, across, from_left]


def scatter4(pieces, axis):
    right = send(pieces[1], axis, 1)
    left = send(pieces[3], axis, 3)
    across = send(pieces[2], axis, 2)
    return [pieces[0], right, across, left]


def after(value, *events):
    return lax.optimization_barrier((value, *events))[0]


def total(parts):
    result = parts[0].astype(F32)
    for part in parts[1:]:
        result = result + part.astype(F32)
    return result


def nt(left, right):
    return lax.dot_general(left, right, (((1,), (1,)), ((), ())), preferred_element_type=F32)


def tn(left, right):
    return lax.dot_general(left, right, (((0,), (0,)), ((), ())), preferred_element_type=F32)


def nn(left, right):
    return jnp.dot(left, right, preferred_element_type=F32)


def at(stack, *index):
    rest = stack.shape[len(index) :]
    piece = lax.dynamic_slice(
        stack, tuple(index) + (0,) * len(rest), (1,) * len(index) + rest
    )
    return piece.reshape(rest)


def adam_update(weight, moment, second, gradient):
    moment_next = beta_one * moment + (1.0 - beta_one) * gradient
    second_next = beta_two * second + (1.0 - beta_two) * gradient * gradient
    corrected = moment_next / (1.0 - beta_one**adam_count)
    scaled = jnp.sqrt(second_next / (1.0 - beta_two**adam_count)) + epsilon
    weight_next = (weight.astype(F32) - learn_rate * corrected / scaled).astype(BF16)
    return (weight_next, moment_next, second_next)


def attention_kernel(at_ref, qg_ref, kv_ref, do_ref, dkv_ref, kt, vt, dkt, dvt):
    y_at, zlo_at, zhi_at = at_ref[0], at_ref[1], at_ref[2]

    def places():
        for y_source in range(4):
            rows = pl.ds((y_source % 2) * 64, 64)
            near = lax.rem(y_source - y_at + 4, 4)
            for zlo in range(2):
                for half in range(2):
                    for step in range(4):
                        block = ((y_source + step) % 4) * 2 + zlo
                        there = pl.ds(block * 256 + half * 128, 128)
                        here = pl.ds((half * 4 + step) * 128, 128)
                        yield y_source, near, zlo, rows, there, here

    for y_source, near, zlo, rows, there, here in places():
        target = kt if y_source < 2 else vt
        target[rows, there] = kv_ref[near, zlo, :, here]

    def stacked(first, last, side):
        low, high = slice(side, side + HD), slice(side + HD, side + 2 * HD)
        return jnp.concatenate([first[:, low], first[:, high], last[:, low], last[:, high]], axis=0)

    row_id = lax.broadcasted_iota(jnp.int32, (128, 1), 0)
    for block in (3, 2, 1, 0):
        keys = (2 * block + 2) * 256
        step = lax.rem(block - y_at + 4, 4)
        first, last = qg_ref[step], qg_ref[4 + step]
        query, grad = stacked(first, last, 0), stacked(first, last, 2 * HD)
        key_t, value_t = kt[:, :keys], vt[:, :keys]
        query_pos = (2 * block + zlo_at) * 256 + (row_id // 64) * 128 + zhi_at * 32 + row_id % 32
        key_pos = lax.broadcasted_iota(jnp.int32, (128, keys), 1)
        scores = nn(query, key_t) * SCALE
        raised = jnp.where(key_pos <= query_pos, jnp.exp(scores), 0.0)
        probs = raised * (1.0 / jnp.sum(raised, axis=1, keepdims=True))
        probs_low = probs.astype(BF16)
        out = nt(probs_low, value_t).astype(BF16)
        prob_grads = nn(grad, value_t)
        delta = jnp.sum(probs * prob_grads, axis=1, keepdims=True)
        score_grads = (probs * (prob_grads - delta)).astype(BF16)
        grad_query = (nt(score_grads, key_t) * SCALE).astype(BF16)
        key_part = tn(query, score_grads)
        value_part = tn(grad, probs_low)
        if block == 3:
            dkt[...] = key_part
            dvt[...] = value_part
        else:
            dkt[:, :keys] += key_part
            dvt[:, :keys] += value_part
        do_ref[step] = jnp.concatenate(
            [grad_query[:32], grad_query[32:64], out[:32], out[32:64]], axis=1
        )
        do_ref[4 + step] = jnp.concatenate(
            [grad_query[64:96], grad_query[96:], out[64:96], out[96:]], axis=1
        )

    for y_source, near, zlo, rows, there, here in places():
        if y_source < 2:
            dkv_ref[near, zlo, :, here] = (dkt[rows, there] * SCALE).astype(BF16)
        else:
            dkv_ref[near, zlo, :, here] = dvt[rows, there].astype(BF16)


def attention(place, queries_grads, keyval):
    return pl.pallas_call(
        attention_kernel,
        out_shape=(
            jax.ShapeDtypeStruct(queries_grads.shape, BF16),
            jax.ShapeDtypeStruct(keyval.shape, BF16),
        ),
        in_specs=[
            pl.BlockSpec(memory_space=pltpu.SMEM),
            pl.BlockSpec(memory_space=pltpu.VMEM),
            pl.BlockSpec(memory_space=pltpu.VMEM),
        ],
        out_specs=[pl.BlockSpec(memory_space=pltpu.VMEM)] * 2,
        scratch_shapes=[
            pltpu.VMEM((HD, 2048), BF16),
            pltpu.VMEM((HD, 2048), BF16),
            pltpu.VMEM((HD, 2048), F32),
            pltpu.VMEM((HD, 2048), F32),
        ],
        compiler_params=pltpu.CompilerParams(vmem_limit_bytes=28 * 1024 * 1024),
    )(place, queries_grads, keyval)


def on_device(
    inputs,
    query_weight,
    keyval_weight,
    output_weight,
    cotangent,
    query_moment,
    query_second,
    keyval_moment,
    keyval_second,
    output_moment,
    output_second,
):
    x_at, core_at = lax.axis_index("x"), lax.axis_index("core")
    y_at, zlo_at = lax.axis_index("y"), lax.axis_index("zlo")
    zhi_at = lax.axis_index("zhi")
    low = zlo_at == 0

    def mod4(value):
        return lax.rem(value + 4, 4)

    def in_order(own, other):
        return jnp.where(low, own, other), jnp.where(low, other, own)

    def sideways(value):
        return jnp.concatenate([value[:, :HD], value[:, HD:]], axis=0)

    def upright(value):
        half = value.shape[0] // 2
        return jnp.concatenate([value[:half], value[half:]], axis=1)

    first = jnp.concatenate([inputs[:128], cotangent[:128]], axis=0)
    last = jnp.concatenate([inputs[128:], cotangent[128:]], axis=0)
    first_x = jnp.concatenate(gather4(first, "x"), axis=1)
    last_y = gather4(last, "y")
    last_y = jnp.concatenate([p[:128] for p in last_y] + [p[128:] for p in last_y], axis=0)
    first_all = gather4(first_x, "y")
    last_all = gather4(last_y, "x")

    def both_cores(which):
        own = [
            jnp.concatenate([p[128 * which : 128 * (which + 1)] for p in first_all], axis=0),
            jnp.concatenate([p[512 * which : 512 * (which + 1)] for p in last_all], axis=1),
        ]
        return [own, [swap(half, "core") for half in own]]

    feats, cots = both_cores(0), both_cores(1)

    packed = swap(jnp.concatenate([query_weight, sideways(output_weight)], axis=0), "zlo")
    query_pair = jnp.concatenate(in_order(query_weight, packed[:2048]), axis=1)
    keyval_t = keyval_weight.T
    keyval_pair = jnp.concatenate(in_order(keyval_t, swap(keyval_t, "zlo")), axis=0)

    query_stack = query_pair.reshape(4, 2, 256, 256)
    joined_stack = jnp.concatenate([query_pair, keyval_pair.T], axis=1).reshape(4, 2, 256, 320)
    query_rel, keyval_rel, joined = [], [], []
    for side in range(2):
        core = core_at ^ side
        query_rel.append(
            jnp.concatenate([at(query_stack, mod4(x_at + j - 4), core) for j in range(4)], axis=0)
        )
        keyval_rel.append(
            jnp.concatenate(
                [
                    lax.dynamic_slice(
                        keyval_pair, (0, (mod4(x_at + j - 4) * 2 + core) * 256), (64, 256)
                    )
                    for j in range(4)
                ],
                axis=1,
            )
        )
        joined.append(
            lax.dynamic_slice(joined_stack, (0, core, 0, 0), (4, 1, 256, 320)).reshape(4, 256, 320)
        )

    packed = after(packed, *feats[0])
    head_rows = jnp.stack([output_weight, upright(packed[2048:])]).reshape(2, 4, 256, 256)
    came = scatter4(
        [
            lax.dynamic_slice(
                head_rows, (0, mod4(y_at + j - 4), 0, 0), (2, 1, 256, 256)
            ).reshape(2, 256, 256)
            for j in range(4)
        ],
        "y",
    )
    col_stack = jnp.stack([came[0], came[3], came[2], came[1]])
    output_rel = [
        jnp.concatenate(
            [
                at(col_stack, mod4(x_at + j - y_at), core_at ^ side ^ zlo_at)
                for j in range(4)
            ],
            axis=1,
        )
        for side in range(2)
    ]

    keyval_part = jnp.concatenate(
        [
            nt(keyval_rel[0], feats[0][half]) + nt(keyval_rel[1], feats[1][half])
            for half in range(2)
        ],
        axis=1,
    ).astype(BF16)
    keyval_own = total(gather4(keyval_part, "zhi")).astype(BF16)
    keyval_both = jnp.stack(in_order(keyval_own, swap(keyval_own, "zlo")))
    keyval_all = jnp.stack(gather4(keyval_both, "y"))

    parts = []
    for half in range(2):
        parts.append(
            jnp.concatenate(
                [
                    nn(feats[0][half], query_rel[0]) + nn(feats[1][half], query_rel[1]),
                    nt(cots[0][half], output_rel[0]) + nt(cots[1][half], output_rel[1]),
                ],
                axis=1,
            )
        )
    parts = jnp.stack(parts).reshape(8, 4, 32, 512)
    pieces = []
    for j in range(4):
        piece = lax.dynamic_slice(parts, (0, mod4(zhi_at + j - 4), 0, 0), (8, 1, 32, 512))
        piece = piece.reshape(8, 32, 512)
        pieces.append(piece if j == 0 else piece.astype(BF16))
    queries_grads = total(scatter4(pieces, "zhi")).astype(BF16)

    place = jnp.stack([y_at, zlo_at, zhi_at]).astype(jnp.int32)
    grads_outs, keyval_parts = attention(place, queries_grads, keyval_all)

    keyval_came = total(scatter4([keyval_parts[j] for j in range(4)], "y")).astype(BF16)
    keyval_kept = jnp.where(low, keyval_came[0], keyval_came[1])
    keyval_sent = jnp.where(low, keyval_came[1], keyval_came[0])
    near = jnp.stack(gather4(grads_outs, "zhi"))
    rows = jnp.stack([at(near, mod4(d - zhi_at)) for d in range(4)], axis=1)
    rows = rows.reshape(2, 512, 512)
    keyval_sum = total([keyval_kept, swap(keyval_sent, "zlo")]).astype(BF16)
    keyval_grads = total(gather4(keyval_sum, "zhi")).astype(BF16)

    both = jnp.concatenate(
        [rows[:, :, : 2 * HD].reshape(2, 4, 128, 256), keyval_grads.T.reshape(2, 4, 128, 64)],
        axis=3,
    )
    both = jnp.concatenate(
        [
            lax.dynamic_slice(both, (0, mod4(j - y_at), 0, 0), (2, 1, 128, 320)).reshape(256, 320)
            for j in range(4)
        ],
        axis=0,
    )
    theirs = [swap(nt(both, joined[1][x]).astype(BF16), "core") for x in range(4)]
    sums = jnp.stack(
        [(nt(both, joined[0][x]) + theirs[x].astype(F32)).astype(BF16) for x in range(4)]
    )
    came = lax.all_to_all(sums.reshape(16, 256, 256), ("x", "y"), 0, 0, tiled=True)
    grad_input = jnp.sum(came.astype(F32), axis=0).astype(BF16)

    query_parts, output_parts = [], []
    for side in range(2):
        part = tn(feats[side][0], rows[0, :, : 2 * HD]) + tn(feats[side][1], rows[1, :, : 2 * HD])
        query_parts.append(part.astype(BF16))
        part = tn(rows[0, :, 2 * HD :], cots[side][0]) + tn(rows[1, :, 2 * HD :], cots[side][1])
        part = part.astype(BF16)
        output_parts.append(jnp.stack([part[:, 256 * j : 256 * (j + 1)] for j in range(4)]))
    query_parts = jnp.concatenate(query_parts, axis=0)
    query_kept = jnp.where(low, query_parts[:, :HD], query_parts[:, HD:])
    query_sent = jnp.where(low, query_parts[:, HD:], query_parts[:, :HD])
    output_parts = jnp.stack(output_parts)
    mine = core_at ^ zlo_at
    output_kept = at(output_parts, mine).reshape(1024, 256)
    output_sent = at(output_parts, mine ^ 1).reshape(1024, 256)
    packed = jnp.concatenate([query_sent, sideways(output_sent)], axis=0)
    packed = swap(after(packed, keyval_grads), "zlo")
    query_sum = total([query_kept, packed[:2048]]).reshape(2, 4, 256, HD)
    query_gradient = jnp.concatenate(
        [at(query_sum, core_at ^ c, mod4(j - x_at)) for j in range(4) for c in range(2)], axis=0
    )
    output_sum = total([output_kept, upright(packed[2048:])]).astype(BF16).reshape(4, 256, 256)
    came = scatter4([at(output_sum, mod4(y_at + j - x_at)) for j in range(4)], "y")
    came = jnp.stack([came[0], came[3], came[2], came[1]])
    output_gradient = jnp.concatenate([at(came, mod4(j - y_at)) for j in range(4)], axis=0)

    keyval_halves = [keyval_grads[:, :512], keyval_grads[:, 512:]]
    keyval_grad_parts = []
    for side in range(2):
        keyval_grad_parts.append(
            (
                nn(keyval_halves[0], feats[side][0]) + nn(keyval_halves[1], feats[side][1])
            ).astype(BF16)
        )
    keyval_grad_parts = jnp.concatenate(keyval_grad_parts, axis=1)
    keyval_kept = jnp.where(low, keyval_grad_parts[:32], keyval_grad_parts[32:])
    keyval_sent = jnp.where(low, keyval_grad_parts[32:], keyval_grad_parts[:32])
    keyval_total = keyval_kept.astype(F32) + swap(keyval_sent, "zlo").astype(F32)
    keyval_gradient = jnp.concatenate(
        [
            lax.dynamic_slice(
                keyval_total, (0, ((core_at ^ c) * 4 + mod4(j - x_at)) * 256), (32, 256)
            )
            for j in range(4)
            for c in range(2)
        ],
        axis=1,
    ).T

    query_next = adam_update(query_weight, query_moment, query_second, query_gradient)
    keyval_next = adam_update(keyval_weight, keyval_moment, keyval_second, keyval_gradient)
    output_next = adam_update(
        output_weight, output_moment, output_second, output_gradient.astype(F32)
    )
    return (grad_input, *query_next, *keyval_next, *output_next)


def solution(mesh):
    fine = Mesh(mesh.devices.reshape(SIZES), NAMES)
    tokens = P(("y", "zlo"), ("zhi", "x", "core"))
    heads = P("zhi", ("x", "core", "y", "zlo"))
    output = P(("x", "core"), ("zhi", "y", "zlo"))
    return jax.shard_map(
        on_device,
        mesh=fine,
        in_specs=(tokens, heads, heads, output, tokens, *[heads] * 4, output, output),
        out_specs=(tokens, *[heads] * 6, *[output] * 3),
        check_vma=False,
    )
```

```python
import math

import jax
import jax.numpy as jnp
from jax import lax
from jax.experimental import pallas as pl
from jax.experimental.pallas import tpu as pltpu
from jax.sharding import Mesh
from jax.sharding import PartitionSpec as P

HD = 128
SCALE = 1.0 / math.sqrt(HD)
F32 = jnp.float32
BF16 = jnp.bfloat16

beta_one = 0.9
beta_two = 0.95
learn_rate = 0.001
adam_count = 100
epsilon = 1e-08

SIZES = (4, 2, 4, 2, 4)
NAMES = ("x", "core", "y", "zlo", "zhi")


def send(value, axis, step):
    return lax.ppermute(value, axis, [(i, (i + step) % 4) for i in range(4)])


def swap(value, axis):
    return lax.ppermute(value, axis, [(0, 1), (1, 0)])


def gather4(value, axis):
    from_left = send(value, axis, 1)
    from_right = send(value, axis, 3)
    across = send(value, axis, 2)
    return [value, from_right, across, from_left]


def scatter4(pieces, axis):
    right = send(pieces[1], axis, 1)
    left = send(pieces[3], axis, 3)
    across = send(pieces[2], axis, 2)
    return [pieces[0], right, across, left]


def after(value, *events):
    return lax.optimization_barrier((value, *events))[0]


def total(parts):
    result = parts[0].astype(F32)
    for part in parts[1:]:
        result = result + part.astype(F32)
    return result


def nt(left, right):
    return lax.dot_general(left, right, (((1,), (1,)), ((), ())), preferred_element_type=F32)


def tn(left, right):
    return lax.dot_general(left, right, (((0,), (0,)), ((), ())), preferred_element_type=F32)


def nn(left, right):
    return jnp.dot(left, right, preferred_element_type=F32)


def at(stack, *index):
    rest = stack.shape[len(index) :]
    piece = lax.dynamic_slice(
        stack, tuple(index) + (0,) * len(rest), (1,) * len(index) + rest
    )
    return piece.reshape(rest)


def adam_update(weight, moment, second, gradient):
    moment_next = beta_one * moment + (1.0 - beta_one) * gradient
    second_next = beta_two * second + (1.0 - beta_two) * gradient * gradient
    corrected = moment_next / (1.0 - beta_one**adam_count)
    scaled = jnp.sqrt(second_next / (1.0 - beta_two**adam_count)) + epsilon
    weight_next = (weight.astype(F32) - learn_rate * corrected / scaled).astype(BF16)
    return (weight_next, moment_next, second_next)


def attention_kernel(at_ref, qg_ref, kv0, kv1, kv2, kv3, do_ref, dkv0, dkv1, dkv2, dkv3, kvt, dkvt):
    y_at, zlo_at, zhi_at = at_ref[0], at_ref[1], at_ref[2]

    def places():
        for near in range(4):
            y_source = lax.rem(y_at + near, 4)
            rows = pl.ds(pl.multiple_of(lax.rem(y_source, 2) * 64, 64), 64)
            for zlo in range(2):
                for y in range(4):
                    yield near, zlo, y, y_source // 2, rows, pl.ds((2 * y + zlo) * 256, 256)

    kv_refs, dkv_refs = (kv0, kv1, kv2, kv3), (dkv0, dkv1, dkv2, dkv3)
    for near, zlo, y, which, rows, there in places():
        kvt[which, rows, there] = kv_refs[near][zlo, y]

    row_id = lax.broadcasted_iota(jnp.int32, (128, 1), 0)
    for block in (3, 2, 1, 0):
        keys = (2 * block + 2) * 256
        first, last = [
            total([qg_ref[depth, which, block] for depth in range(4)]).astype(BF16)
            for which in range(2)
        ]
        query = jnp.concatenate([first[:, :HD], first[:, HD:]], axis=0)
        grad = jnp.concatenate([last[:, :HD], last[:, HD:]], axis=0)
        key_t, value_t = kvt[0, :, :keys], kvt[1, :, :keys]
        query_pos = (2 * block + zlo_at) * 256 + zhi_at * 64 + row_id % 64
        key_pos = lax.broadcasted_iota(jnp.int32, (128, keys), 1)
        scores = nn(query, key_t) * SCALE
        raised = jnp.where(key_pos <= query_pos, jnp.exp(scores), 0.0)
        probs = raised * (1.0 / jnp.sum(raised, axis=1, keepdims=True))
        probs_low = probs.astype(BF16)
        out = nt(probs_low, value_t).astype(BF16)
        prob_grads = nn(grad, value_t)
        delta = jnp.sum(probs * prob_grads, axis=1, keepdims=True)
        score_grads = (probs * (prob_grads - delta)).astype(BF16)
        grad_query = (nt(score_grads, key_t) * SCALE).astype(BF16)
        key_part = tn(query, score_grads) * SCALE
        value_part = tn(grad, probs_low)
        if block == 3:
            dkvt[0] = key_part
            dkvt[1] = value_part
        else:
            dkvt[0, :, :keys] += key_part
            dkvt[1, :, :keys] += value_part
        do_ref[0, block] = jnp.concatenate([grad_query[:64], grad_query[64:]], axis=1)
        do_ref[1, block] = jnp.concatenate([out[:64], out[64:]], axis=1)

    for near, zlo, y, which, rows, there in places():
        dkv_refs[near][zlo, y] = dkvt[which, rows, there].astype(BF16)


def attention(place, queries_grads, keyvals):
    vmem = pl.BlockSpec(memory_space=pltpu.VMEM)
    return pl.pallas_call(
        attention_kernel,
        out_shape=[jax.ShapeDtypeStruct(queries_grads.shape[1:], BF16)]
        + [jax.ShapeDtypeStruct(part.shape, BF16) for part in keyvals],
        in_specs=[pl.BlockSpec(memory_space=pltpu.SMEM)] + [vmem] * 5,
        out_specs=[vmem] * 5,
        scratch_shapes=[pltpu.VMEM((2, HD, 2048), BF16), pltpu.VMEM((2, HD, 2048), F32)],
        compiler_params=pltpu.CompilerParams(vmem_limit_bytes=28 * 1024 * 1024),
    )(place, queries_grads, *keyvals)


def block(x, y):
    return x * 4 + y


def part(x):
    return pl.ds(x * 256, 256)


def keyval_kernel(tokens, keyval, own, other):
    for y in range(4):
        result = nt(keyval[:, part(0)], tokens[block(0, y)])
        for x in range(1, 4):
            result += nt(keyval[:, part(x)], tokens[block(x, y)])
        result = result.astype(BF16)
        own[y] = result[:64]
        other[y] = result[64:]


def query_kernel(feats, cots, query, output, own, other):
    for y in range(4):
        queries = nn(feats[block(0, y)], query[part(0), :])
        grads = nt(cots[block(0, y)], output[:, part(0)])
        for x in range(1, 4):
            queries += nn(feats[block(x, y)], query[part(x), :])
            grads += nt(cots[block(x, y)], output[:, part(x)])
        for which, value in enumerate((queries.astype(BF16), grads.astype(BF16))):
            for core, ref in enumerate((own, other)):
                for depth in range(4):
                    ref[depth, which, y] = value[
                        depth * 64 : (depth + 1) * 64, core * 256 : (core + 1) * 256
                    ]


def rows_of(place, ref, which, y):
    near = [lax.rem(depth - place[2] + 4, 4) for depth in range(4)]
    return jnp.concatenate([ref[n, which, y] for n in near], axis=0)


def input_grad_kernel(place, grads, grads_other, kv, kv_other, query, keyval, out):
    for y in range(4):
        result = nt(rows_of(place, grads, 0, y), query[:, :256])
        result += nt(rows_of(place, grads_other, 0, y), query[:, 256:])
        result += tn(jnp.concatenate([kv[y], kv_other[y]], axis=0), keyval[...])
        result = result.astype(BF16)
        for x in range(4):
            out[block(x, y)] = result[:, x * 256 : (x + 1) * 256]


def weight_grad_kernel(place, *refs):
    feats, cots, grads, grads_other, query, query_other, output, output_other = refs
    right, left = [
        [
            jnp.concatenate(
                [rows_of(place, grads, which, y), rows_of(place, grads_other, which, y)], axis=1
            )
            for y in range(4)
        ]
        for which in range(2)
    ]
    for x in range(4):
        result = tn(feats[block(x, 0)], right[0])
        for y in range(1, 4):
            result += tn(feats[block(x, y)], right[y])
        query[x] = result[:, :256].astype(BF16)
        query_other[x] = result[:, 256:].astype(BF16)
        result = tn(left[0], cots[block(x, 0)])
        for y in range(1, 4):
            result += tn(left[y], cots[block(x, y)])
        output[x] = result[:256].astype(BF16)
        output_other[x] = result[256:].astype(BF16)


def keyval_grad_kernel(tokens, kv, kv_other, own, other):
    left = [jnp.concatenate([kv[y], kv_other[y]], axis=0) for y in range(4)]
    for x in range(4):
        result = nn(left[0], tokens[block(x, 0)])
        for y in range(1, 4):
            result += nn(left[y], tokens[block(x, y)])
        own[:, part(x)] = result[:64].astype(BF16)
        other[:, part(x)] = result[64:].astype(BF16)


def on_chip(kernel, shapes, *operands):
    result = pl.pallas_call(
        kernel,
        out_shape=tuple(jax.ShapeDtypeStruct(shape, BF16) for shape in shapes),
        in_specs=[
            pl.BlockSpec(memory_space=pltpu.SMEM if operand.ndim == 1 else pltpu.VMEM)
            for operand in operands
        ],
        out_specs=tuple(pl.BlockSpec(memory_space=pltpu.VMEM) for _ in shapes),
        compiler_params=pltpu.CompilerParams(vmem_limit_bytes=28 * 1024 * 1024),
    )(*operands)
    return result


def on_device(
    inputs,
    query_weight,
    keyval_weight,
    output_weight,
    cotangent,
    query_moment,
    query_second,
    keyval_moment,
    keyval_second,
    output_moment,
    output_second,
):
    x_at, core_at = lax.axis_index("x"), lax.axis_index("core")
    y_at, zlo_at = lax.axis_index("y"), lax.axis_index("zlo")
    zhi_at = lax.axis_index("zhi")
    low = zlo_at == 0

    def mod4(value):
        return lax.rem(value + 4, 4)

    def in_order(own, other):
        return jnp.where(low, own, other), jnp.where(low, other, own)

    def sideways(value):
        return jnp.concatenate([value[:, :HD], value[:, HD:]], axis=0)

    def upright(value):
        half = value.shape[0] // 2
        return jnp.concatenate([value[:half], value[half:]], axis=1)

    def core_swap(value):
        return swap(value, "core")

    place = jnp.stack([y_at, zlo_at, zhi_at]).astype(jnp.int32)

    cots = lax.all_gather(cotangent, ("x", "y"), axis=0, tiled=True).reshape(16, 256, 256)
    feats = lax.all_to_all(
        jnp.broadcast_to(inputs[None], (16, 256, 256)), ("x", "y"), 0, 0, tiled=True
    )

    packed = swap(jnp.concatenate([query_weight, sideways(output_weight)], axis=0), "zlo")
    query_pair = jnp.concatenate(in_order(query_weight, packed[:2048]), axis=1)
    query_pair = query_pair.reshape(4, 2, 256, 256)
    keyval_t = keyval_weight.T
    keyval_pair = jnp.concatenate(in_order(keyval_t, swap(keyval_t, "zlo")), axis=0)

    def query_rows_of(core):
        return lax.dynamic_slice(query_pair, (0, core, 0, 0), (4, 1, 256, 256)).reshape(1024, 256)

    def keyval_columns_of(core):
        return jnp.concatenate(
            [
                lax.dynamic_slice(keyval_pair, (0, (2 * x + core) * 256), (64, 256))
                for x in range(4)
            ],
            axis=1,
        )

    query_both = jnp.concatenate(
        [query_rows_of(core_at), core_swap(query_rows_of(1 - core_at))], axis=1
    )
    keyval_both = jnp.concatenate(
        [keyval_columns_of(core_at), core_swap(keyval_columns_of(1 - core_at))], axis=0
    )

    own, other = on_chip(keyval_kernel, ((4, 64, 256), (4, 64, 256)), feats, keyval_both)
    own = total([own, core_swap(other)]).astype(BF16)
    keyval_own = total(gather4(own, "zhi")).astype(BF16)
    keyval_here = jnp.stack(in_order(keyval_own, swap(keyval_own, "zlo")))
    keyval_all = gather4(keyval_here, "y")

    packed = after(packed, feats)
    head_rows = jnp.stack([output_weight, upright(packed[2048:])]).reshape(2, 4, 256, 256)
    came = scatter4(
        [
            lax.dynamic_slice(
                head_rows, (0, mod4(y_at + j - 4), 0, 0), (2, 1, 256, 256)
            ).reshape(2, 256, 256)
            for j in range(4)
        ],
        "y",
    )
    came = lax.optimization_barrier((*came, keyval_own))[:4]
    col_stack = jnp.stack([came[0], came[3], came[2], came[1]])

    def output_columns_of(core):
        return jnp.concatenate(
            [at(col_stack, mod4(x - y_at), core ^ zlo_at) for x in range(4)], axis=1
        )

    output_both = jnp.concatenate(
        [output_columns_of(core_at), core_swap(output_columns_of(1 - core_at))], axis=0
    )
    cots = after(cots, keyval_here)
    own, other = on_chip(
        query_kernel,
        ((4, 2, 4, 64, 256), (4, 2, 4, 64, 256)),
        feats,
        cots,
        query_both,
        output_both,
    )
    own = total([own, core_swap(other)]).astype(BF16)
    came = lax.all_to_all(own, "zhi", 0, 0, tiled=True)
    grads_outs, *keyval_parts = attention(place, came, keyval_all)

    came = total(scatter4(keyval_parts, "y")).astype(BF16)
    grads = jnp.stack(gather4(grads_outs, "zhi"))
    grads_other = core_swap(grads)
    came = total([at(came, zlo_at), swap(at(came, 1 - zlo_at), "zlo")]).astype(BF16)
    keyval_grads = total(gather4(came, "zhi")).astype(BF16)

    own, other, output_own, output_other = on_chip(
        weight_grad_kernel, ((4, 256, 256),) * 4, place, feats, cots, grads, grads_other
    )
    keyval_grads, own = lax.optimization_barrier((keyval_grads, own))
    keyval_grads_other = core_swap(keyval_grads)
    query_parts = jnp.concatenate([own, core_swap(other)], axis=0).reshape(2048, 256)
    query_kept = jnp.where(low, query_parts[:, :HD], query_parts[:, HD:])
    query_sent = jnp.where(low, query_parts[:, HD:], query_parts[:, :HD])
    query_came = swap(after(query_sent, keyval_grads), "zlo")
    output_parts = jnp.stack([output_own, core_swap(output_other)])
    mine = core_at ^ zlo_at
    output_came = swap(after(at(output_parts, mine ^ 1), keyval_grads), "zlo")

    sums = on_chip(
        input_grad_kernel,
        ((16, 256, 256),),
        place,
        grads,
        grads_other,
        keyval_grads,
        keyval_grads_other,
        query_both,
        keyval_both,
    )[0]
    came = lax.all_to_all(sums, ("x", "y"), 0, 0, tiled=True)
    grad_input = jnp.sum(came.astype(F32), axis=0).astype(BF16)

    query_sum = total([query_kept, query_came]).reshape(2, 4, 256, HD)
    query_gradient = jnp.concatenate(
        [at(query_sum, core_at ^ c)[x] for x in range(4) for c in range(2)], axis=0
    )

    output_sum = total([at(output_parts, mine), after(output_came, query_came)]).astype(BF16)
    came = scatter4([at(output_sum, mod4(y_at + j - 4)) for j in range(4)], "y")
    came = jnp.stack([came[0], came[3], came[2], came[1]])
    output_gradient = jnp.concatenate([at(came, mod4(j - y_at)) for j in range(4)], axis=0)

    own, other = on_chip(
        keyval_grad_kernel,
        ((64, 1024), (64, 1024)),
        feats,
        keyval_grads,
        after(keyval_grads_other, sums, query_came),
    )
    keyval_parts = jnp.concatenate([own, core_swap(other)], axis=1)
    keyval_kept = jnp.where(low, keyval_parts[:32], keyval_parts[32:])
    keyval_sent = jnp.where(low, keyval_parts[32:], keyval_parts[:32])
    keyval_total = total([keyval_kept, swap(keyval_sent, "zlo")])
    keyval_gradient = jnp.concatenate(
        [
            lax.dynamic_slice(keyval_total, (0, ((core_at ^ c) * 4 + x) * 256), (32, 256))
            for x in range(4)
            for c in range(2)
        ],
        axis=1,
    ).T

    query_next = adam_update(query_weight, query_moment, query_second, query_gradient)
    keyval_next = adam_update(keyval_weight, keyval_moment, keyval_second, keyval_gradient)
    output_next = adam_update(
        output_weight, output_moment, output_second, output_gradient.astype(F32)
    )
    return (grad_input, *query_next, *keyval_next, *output_next)


def solution(mesh):
    fine = Mesh(mesh.devices.reshape(SIZES), NAMES)
    tokens = P(("y", "zlo"), ("zhi", "x", "core"))
    heads = P("zhi", ("x", "core", "y", "zlo"))
    output = P(("x", "core"), ("zhi", "y", "zlo"))
    return jax.shard_map(
        on_device,
        mesh=fine,
        in_specs=(tokens, heads, heads, output, tokens, *[heads] * 4, output, output),
        out_specs=(tokens, *[heads] * 6, *[output] * 3),
        check_vma=False,
    )
```

```python
import math

import jax
import jax.numpy as jnp
from jax import lax
from jax.experimental import pallas as pl
from jax.experimental.pallas import tpu as pltpu
from jax.sharding import Mesh
from jax.sharding import PartitionSpec as P

HD = 128
SCALE = 1.0 / math.sqrt(HD)
F32 = jnp.float32
BF16 = jnp.bfloat16

beta_one = 0.9
beta_two = 0.95
learn_rate = 0.001
adam_count = 100
epsilon = 1e-08

SIZES = (4, 2, 4, 2, 4)
NAMES = ("x", "core", "y", "zlo", "zhi")


def send(value, axis, step):
    return lax.ppermute(value, axis, [(i, (i + step) % 4) for i in range(4)])


def swap(value, axis):
    return lax.ppermute(value, axis, [(0, 1), (1, 0)])


def gather4(value, axis):
    from_left = send(value, axis, 1)
    from_right = send(value, axis, 3)
    across = send(value, axis, 2)
    return [value, from_right, across, from_left]


def scatter4(pieces, axis):
    right = send(pieces[1], axis, 1)
    left = send(pieces[3], axis, 3)
    across = send(pieces[2], axis, 2)
    return [pieces[0], right, across, left]


def after(value, *events):
    return lax.optimization_barrier((value, *events))[0]


def total(parts):
    result = parts[0].astype(F32)
    for part in parts[1:]:
        result = result + part.astype(F32)
    return result


def nt(left, right):
    return lax.dot_general(left, right, (((1,), (1,)), ((), ())), preferred_element_type=F32)


def tn(left, right):
    return lax.dot_general(left, right, (((0,), (0,)), ((), ())), preferred_element_type=F32)


def nn(left, right):
    return jnp.dot(left, right, preferred_element_type=F32)


def at(stack, *index):
    rest = stack.shape[len(index) :]
    piece = lax.dynamic_slice(
        stack, tuple(index) + (0,) * len(rest), (1,) * len(index) + rest
    )
    return piece.reshape(rest)


def adam_update(weight, moment, second, gradient):
    moment_next = beta_one * moment + (1.0 - beta_one) * gradient
    second_next = beta_two * second + (1.0 - beta_two) * gradient * gradient
    corrected = moment_next / (1.0 - beta_one**adam_count)
    scaled = jnp.sqrt(second_next / (1.0 - beta_two**adam_count)) + epsilon
    weight_next = (weight.astype(F32) - learn_rate * corrected / scaled).astype(BF16)
    return (weight_next, moment_next, second_next)


def attention_kernel(at_ref, qg_ref, kv0, kv1, kv2, kv3, do_ref, dkv0, dkv1, dkv2, dkv3, kvt, dkvt):
    y_at, zlo_at, zhi_at = at_ref[0], at_ref[1], at_ref[2]

    def places():
        for near in range(4):
            y_source = lax.rem(y_at + near, 4)
            rows = pl.ds(pl.multiple_of(lax.rem(y_source, 2) * 64, 64), 64)
            for zlo in range(2):
                for y in range(4):
                    yield near, zlo, y, y_source // 2, rows, pl.ds((2 * y + zlo) * 256, 256)

    kv_refs, dkv_refs = (kv0, kv1, kv2, kv3), (dkv0, dkv1, dkv2, dkv3)
    for near, zlo, y, which, rows, there in places():
        kvt[which, rows, there] = kv_refs[near][zlo, y]

    row_id = lax.broadcasted_iota(jnp.int32, (128, 1), 0)
    for block in (3, 2, 1, 0):
        keys = (2 * block + 2) * 256
        first, last = [
            total([qg_ref[depth, which, block] for depth in range(4)]).astype(BF16)
            for which in range(2)
        ]
        query = jnp.concatenate([first[:, :HD], first[:, HD:]], axis=0)
        grad = jnp.concatenate([last[:, :HD], last[:, HD:]], axis=0)
        key_t, value_t = kvt[0, :, :keys], kvt[1, :, :keys]
        query_pos = (2 * block + zlo_at) * 256 + zhi_at * 64 + row_id % 64
        key_pos = lax.broadcasted_iota(jnp.int32, (128, keys), 1)
        scores = nn(query, key_t) * SCALE
        raised = jnp.where(key_pos <= query_pos, jnp.exp(scores), 0.0)
        probs = raised * (1.0 / jnp.sum(raised, axis=1, keepdims=True))
        probs_low = probs.astype(BF16)
        out = nt(probs_low, value_t).astype(BF16)
        prob_grads = nn(grad, value_t)
        delta = jnp.sum(probs * prob_grads, axis=1, keepdims=True)
        score_grads = (probs * (prob_grads - delta)).astype(BF16)
        grad_query = (nt(score_grads, key_t) * SCALE).astype(BF16)
        key_part = tn(query, score_grads) * SCALE
        value_part = tn(grad, probs_low)
        if block == 3:
            dkvt[0] = key_part
            dkvt[1] = value_part
        else:
            dkvt[0, :, :keys] += key_part
            dkvt[1, :, :keys] += value_part
        do_ref[0, block] = jnp.concatenate([grad_query[:64], grad_query[64:]], axis=1)
        do_ref[1, block] = jnp.concatenate([out[:64], out[64:]], axis=1)

    for near, zlo, y, which, rows, there in places():
        dkv_refs[near][zlo, y] = dkvt[which, rows, there].astype(BF16)


def attention(place, queries_grads, keyvals):
    vmem = pl.BlockSpec(memory_space=pltpu.VMEM)
    return pl.pallas_call(
        attention_kernel,
        out_shape=[jax.ShapeDtypeStruct(queries_grads.shape[1:], BF16)]
        + [jax.ShapeDtypeStruct(part.shape, BF16) for part in keyvals],
        in_specs=[pl.BlockSpec(memory_space=pltpu.SMEM)] + [vmem] * 5,
        out_specs=[vmem] * 5,
        scratch_shapes=[pltpu.VMEM((2, HD, 2048), BF16), pltpu.VMEM((2, HD, 2048), F32)],
        compiler_params=pltpu.CompilerParams(vmem_limit_bytes=28 * 1024 * 1024),
    )(place, queries_grads, *keyvals)


def block(x, y):
    return x * 4 + y


def part(x):
    return pl.ds(x * 256, 256)


def keyval_kernel(tokens, keyval, own, other):
    for y in range(4):
        result = nt(keyval[:, part(0)], tokens[block(0, y)])
        for x in range(1, 4):
            result += nt(keyval[:, part(x)], tokens[block(x, y)])
        result = result.astype(BF16)
        own[y] = result[:64]
        other[y] = result[64:]


def query_kernel(feats, cots, query, output, own, other):
    for y in range(4):
        queries = nn(feats[block(0, y)], query[part(0), :])
        grads = nt(cots[block(0, y)], output[:, part(0)])
        for x in range(1, 4):
            queries += nn(feats[block(x, y)], query[part(x), :])
            grads += nt(cots[block(x, y)], output[:, part(x)])
        for which, value in enumerate((queries.astype(BF16), grads.astype(BF16))):
            for core, ref in enumerate((own, other)):
                for depth in range(4):
                    ref[depth, which, y] = value[
                        depth * 64 : (depth + 1) * 64, core * 256 : (core + 1) * 256
                    ]


def rows_of(place, ref, y):
    near = [lax.rem(depth - place[2] + 4, 4) for depth in range(4)]
    return jnp.concatenate([ref[n, y] for n in near], axis=0)


def input_grad_kernel(place, grads, grads_other, kv, kv_other, query, keyval, out):
    for y in range(4):
        result = nt(rows_of(place, grads, y), query[:, :256])
        result += nt(rows_of(place, grads_other, y), query[:, 256:])
        result += tn(jnp.concatenate([kv[y], kv_other[y]], axis=0), keyval[...])
        result = result.astype(BF16)
        for x in range(4):
            out[block(x, y)] = result[:, x * 256 : (x + 1) * 256]


def both_rows(place, ref, ref_other):
    return [
        jnp.concatenate([rows_of(place, ref, y), rows_of(place, ref_other, y)], axis=1)
        for y in range(4)
    ]


def query_grad_kernel(place, tokens, grads, grads_other, own, other):
    right = both_rows(place, grads, grads_other)
    for x in range(4):
        result = tn(tokens[block(x, 0)], right[0])
        for y in range(1, 4):
            result += tn(tokens[block(x, y)], right[y])
        own[x] = result[:, :256].astype(BF16)
        other[x] = result[:, 256:].astype(BF16)


def output_grad_kernel(place, tokens, outs, outs_other, own, other):
    left = both_rows(place, outs, outs_other)
    for x in range(4):
        result = tn(left[0], tokens[block(x, 0)])
        for y in range(1, 4):
            result += tn(left[y], tokens[block(x, y)])
        own[x] = result[:256].astype(BF16)
        other[x] = result[256:].astype(BF16)


def keyval_grad_kernel(tokens, kv, kv_other, own, other):
    left = [jnp.concatenate([kv[y], kv_other[y]], axis=0) for y in range(4)]
    for x in range(4):
        result = nn(left[0], tokens[block(x, 0)])
        for y in range(1, 4):
            result += nn(left[y], tokens[block(x, y)])
        own[:, part(x)] = result[:64].astype(BF16)
        other[:, part(x)] = result[64:].astype(BF16)


def on_chip(kernel, shapes, *operands):
    result = pl.pallas_call(
        kernel,
        out_shape=tuple(jax.ShapeDtypeStruct(shape, BF16) for shape in shapes),
        in_specs=[
            pl.BlockSpec(memory_space=pltpu.SMEM if operand.ndim == 1 else pltpu.VMEM)
            for operand in operands
        ],
        out_specs=tuple(pl.BlockSpec(memory_space=pltpu.VMEM) for _ in shapes),
        compiler_params=pltpu.CompilerParams(vmem_limit_bytes=28 * 1024 * 1024),
    )(*operands)
    return result


def on_device(
    inputs,
    query_weight,
    keyval_weight,
    output_weight,
    cotangent,
    query_moment,
    query_second,
    keyval_moment,
    keyval_second,
    output_moment,
    output_second,
):
    x_at, core_at = lax.axis_index("x"), lax.axis_index("core")
    y_at, zlo_at = lax.axis_index("y"), lax.axis_index("zlo")
    zhi_at = lax.axis_index("zhi")
    low = zlo_at == 0

    def mod4(value):
        return lax.rem(value + 4, 4)

    def in_order(own, other):
        return jnp.where(low, own, other), jnp.where(low, other, own)

    def sideways(value):
        return jnp.concatenate([value[:, :HD], value[:, HD:]], axis=0)

    def upright(value):
        half = value.shape[0] // 2
        return jnp.concatenate([value[:half], value[half:]], axis=1)

    def core_swap(value):
        return swap(value, "core")

    place = jnp.stack([y_at, zlo_at, zhi_at]).astype(jnp.int32)

    cots = lax.all_gather(cotangent, ("x", "y"), axis=0, tiled=True).reshape(16, 256, 256)
    feats = lax.all_to_all(
        jnp.broadcast_to(inputs[None], (16, 256, 256)), ("x", "y"), 0, 0, tiled=True
    )

    packed = swap(jnp.concatenate([query_weight, sideways(output_weight)], axis=0), "zlo")
    query_pair = jnp.concatenate(in_order(query_weight, packed[:2048]), axis=1)
    query_pair = query_pair.reshape(4, 2, 256, 256)
    keyval_t = keyval_weight.T
    keyval_pair = jnp.concatenate(in_order(keyval_t, swap(keyval_t, "zlo")), axis=0)

    def query_rows_of(core):
        return lax.dynamic_slice(query_pair, (0, core, 0, 0), (4, 1, 256, 256)).reshape(1024, 256)

    def keyval_columns_of(core):
        return jnp.concatenate(
            [
                lax.dynamic_slice(keyval_pair, (0, (2 * x + core) * 256), (64, 256))
                for x in range(4)
            ],
            axis=1,
        )

    query_both = jnp.concatenate(
        [query_rows_of(core_at), core_swap(query_rows_of(1 - core_at))], axis=1
    )
    keyval_both = jnp.concatenate(
        [keyval_columns_of(core_at), core_swap(keyval_columns_of(1 - core_at))], axis=0
    )

    own, other = on_chip(keyval_kernel, ((4, 64, 256), (4, 64, 256)), feats, keyval_both)
    own = total([own, core_swap(other)]).astype(BF16)
    keyval_own = total(gather4(own, "zhi")).astype(BF16)
    keyval_here = jnp.stack(in_order(keyval_own, swap(keyval_own, "zlo")))
    keyval_all = gather4(keyval_here, "y")

    packed = after(packed, feats)
    head_rows = jnp.stack([output_weight, upright(packed[2048:])]).reshape(2, 4, 256, 256)
    came = scatter4(
        [
            lax.dynamic_slice(
                head_rows, (0, mod4(y_at + j - 4), 0, 0), (2, 1, 256, 256)
            ).reshape(2, 256, 256)
            for j in range(4)
        ],
        "y",
    )
    came = lax.optimization_barrier((*came, keyval_own))[:4]
    col_stack = jnp.stack([came[0], came[3], came[2], came[1]])

    def output_columns_of(core):
        return jnp.concatenate(
            [at(col_stack, mod4(x - y_at), core ^ zlo_at) for x in range(4)], axis=1
        )

    output_both = jnp.concatenate(
        [output_columns_of(core_at), core_swap(output_columns_of(1 - core_at))], axis=0
    )
    cots = after(cots, keyval_here)
    own, other = on_chip(
        query_kernel,
        ((4, 2, 4, 64, 256), (4, 2, 4, 64, 256)),
        feats,
        cots,
        query_both,
        output_both,
    )
    own = total([own, core_swap(other)]).astype(BF16)
    came = lax.all_to_all(own, "zhi", 0, 0, tiled=True)
    grads_outs, *keyval_parts = attention(place, came, keyval_all)

    came = total(scatter4(keyval_parts, "y")).astype(BF16)
    grads = jnp.stack(gather4(grads_outs[0], "zhi"))
    grads_other = core_swap(grads)
    came = total([at(came, zlo_at), swap(at(came, 1 - zlo_at), "zlo")]).astype(BF16)
    keyval_grads = total(gather4(came, "zhi")).astype(BF16)

    shapes = ((4, 256, 256), (4, 256, 256))
    own, other = on_chip(query_grad_kernel, shapes, place, feats, grads, grads_other)
    keyval_grads_other = core_swap(keyval_grads)
    query_parts = jnp.concatenate([own, core_swap(other)], axis=0).reshape(2048, 256)
    query_kept = jnp.where(low, query_parts[:, :HD], query_parts[:, HD:])
    query_sent = jnp.where(low, query_parts[:, HD:], query_parts[:, :HD])
    query_came = swap(query_sent, "zlo")

    sums = on_chip(
        input_grad_kernel,
        ((16, 256, 256),),
        place,
        grads,
        grads_other,
        keyval_grads,
        keyval_grads_other,
        query_both,
        keyval_both,
    )[0]
    came = lax.all_to_all(sums, ("x", "y"), 0, 0, tiled=True)
    grad_input = jnp.sum(came.astype(F32), axis=0).astype(BF16)

    outs = jnp.stack(gather4(after(grads_outs[1], grads), "zhi"))
    outs_other = core_swap(outs)
    own, other = on_chip(
        output_grad_kernel, shapes, place, cots, outs, after(outs_other, sums)
    )
    output_parts = jnp.stack([own, core_swap(other)])
    mine = core_at ^ zlo_at
    output_came = swap(at(output_parts, mine ^ 1), "zlo")
    query_sum = total([query_kept, query_came]).reshape(2, 4, 256, HD)
    query_gradient = jnp.concatenate(
        [at(query_sum, core_at ^ c)[x] for x in range(4) for c in range(2)], axis=0
    )

    output_sum = total([at(output_parts, mine), output_came]).astype(BF16)
    came = scatter4([at(output_sum, mod4(y_at + j - 4)) for j in range(4)], "y")
    came = jnp.stack([came[0], came[3], came[2], came[1]])
    output_gradient = jnp.concatenate([at(came, mod4(j - y_at)) for j in range(4)], axis=0)

    own, other = on_chip(
        keyval_grad_kernel,
        ((64, 1024), (64, 1024)),
        feats,
        keyval_grads,
        after(keyval_grads_other, sums),
    )
    keyval_parts = jnp.concatenate([own, core_swap(other)], axis=1)
    keyval_kept = jnp.where(low, keyval_parts[:32], keyval_parts[32:])
    keyval_sent = jnp.where(low, keyval_parts[32:], keyval_parts[:32])
    keyval_total = total([keyval_kept, swap(keyval_sent, "zlo")])
    keyval_gradient = jnp.concatenate(
        [
            lax.dynamic_slice(keyval_total, (0, ((core_at ^ c) * 4 + x) * 256), (32, 256))
            for x in range(4)
            for c in range(2)
        ],
        axis=1,
    ).T

    query_next = adam_update(query_weight, query_moment, query_second, query_gradient)
    keyval_next = adam_update(keyval_weight, keyval_moment, keyval_second, keyval_gradient)
    output_next = adam_update(
        output_weight, output_moment, output_second, output_gradient.astype(F32)
    )
    return (grad_input, *query_next, *keyval_next, *output_next)


def solution(mesh):
    fine = Mesh(mesh.devices.reshape(SIZES), NAMES)
    tokens = P(("y", "zlo"), ("zhi", "x", "core"))
    heads = P("zhi", ("x", "core", "y", "zlo"))
    output = P(("x", "core"), ("zhi", "y", "zlo"))
    return jax.shard_map(
        on_device,
        mesh=fine,
        in_specs=(tokens, heads, heads, output, tokens, *[heads] * 4, output, output),
        out_specs=(tokens, *[heads] * 6, *[output] * 3),
        check_vma=False,
    )
```
